128 devices in a mesh: row: 8 (over y, core), col: 16 (over z, x).
Axes of the slice: x: 4, y: 4, z: 4, core: 2. Of those that a mesh axis runs over, the one named last changes fastest.
Arguments:
- lower_panel: float32 [7, 8, 2048, 4096], P(None, 'row', 'col'), may hold values from -0.0625 to 0.0625
- test_cross: float32 [7, 8, 2048, 1024], P(None, 'row', 'col'), may hold values from -6 to 6
- diag_inverse: float32 [2, 2048, 2048], P(None, 'col'), may hold values from -2 to 2, as said below
Outputs:
- solved: float32 [7, 8, 2048, 1024], P(None, 'row', 'col')
The draws below stay inside these ranges and needn't reach their ends.
Inputs may be any that keep to these rules, and one draw needn't show every extreme that they name: `diag_inverse`: both matrices are lower triangular with a positive diagonal.
All inputs are finite; a program needn't handle non-finite values.
Results may differ from the reference program's by a relative error of at most 0.0001.
Values sent between devices are 32-bit elements; how exact they have to be, the bound alone decides.
A program may use at most 128 MiB of HBM per device.

```python
import jax
import jax.numpy as jnp
from jax import lax

BS = 2048
TESTS = 1024
RBD = 7
N_ROW = 8


def draw_diag_inverse(key, part):
    key = jax.random.fold_in(key, 7)
    first, second = jax.random.split(key)
    rows = lax.broadcasted_iota(jnp.int32, (2, BS, BS), 1)
    cols = lax.broadcasted_iota(jnp.int32, (2, BS, BS), 2)
    spread_scale = 0.5 / BS ** 0.5
    below = jnp.clip(jax.random.normal(first, (2, BS, BS), jnp.float32), -6.0, 6.0) * spread_scale
    diagonal = jnp.exp(jax.random.uniform(second, (2, BS, BS), jnp.float32, jnp.log(0.5), jnp.log(2.0)))
    return jnp.where(rows > cols, below, jnp.where(rows == cols, diagonal, 0.0))


def level_of(key, dims, shards, least, top_value):
    def one(dim, parts):
        draws = jax.random.uniform(jax.random.fold_in(jax.random.fold_in(key, 6), dim), (parts,), jnp.float32, least / len(shards), top_value / len(shards))
        return jnp.repeat(jnp.exp(draws), dims[dim] // parts).reshape((-1,) + (1,) * (len(dims) - dim - 1))

    level = one(*shards[0])
    for cut in shards[1:]:
        level = level * one(*cut)
    return level


def normal_values(rng, extent, width, bound, shards=(), kind=jnp.bfloat16):
    gain = level_of(rng, extent, shards, -0.22, 0.18) if shards else 1.0
    drawn = jax.random.normal(rng, extent, jnp.float32) * width * gain
    return jnp.minimum(jnp.maximum(drawn, -bound), bound).astype(kind)


def setup_inputs(seed: int = 0) -> dict:
    key_list = jax.random.split(jax.random.key(seed), 4)
    lower_panel = normal_values(key_list[0], (RBD, N_ROW, BS, 2 * BS), (4 * BS) ** -0.5, 0.0625, ((1, 8), (2, 16)), jnp.float32)
    test_cross = normal_values(key_list[1], (RBD, N_ROW, BS, TESTS), 1.0, 6.0, ((1, 8), (2, 16)), jnp.float32)
    diag_inverse = draw_diag_inverse(jax.random.fold_in(key_list[3], 71), 0)
    return dict(lower_panel=lower_panel, test_cross=test_cross, diag_inverse=diag_inverse)


def reference(lower_panel, test_cross, diag_inverse):
    count = RBD * N_ROW
    panel = lower_panel.reshape(count, BS, 2 * BS)
    state = test_cross.reshape(count, BS, TESTS)
    index = jnp.arange(count, dtype=jnp.int32)
    answers = []
    for step in range(2):
        block_solve = jnp.dot(diag_inverse[step], state[step], precision=lax.Precision.HIGHEST, preferred_element_type=jnp.float32)
        answers.append(block_solve)
        update = jnp.einsum("abk,kt->abt", panel[:, :, step * BS:(step + 1) * BS], block_solve, precision=lax.Precision.HIGHEST, preferred_element_type=jnp.float32)
        state = jnp.where((index > step)[:, None, None], state - update, state)
    state = state.at[0].set(answers[0]).at[1].set(answers[1])
    return state.reshape(RBD, N_ROW, BS, TESTS)
```

```python
import functools

import jax
import jax.numpy as jnp
from jax import lax
from jax.experimental import pallas as pl
from jax.experimental.pallas import tpu as pltpu
from jax.sharding import PartitionSpec as P

MESH = pl.DeviceIdType.MESH
DMA = pltpu.SemaphoreType.DMA
F32 = jnp.float32
BF16 = jnp.bfloat16
NEAR = 48


def split(value):
    high = value.astype(BF16)
    return high, (value - high.astype(F32)).astype(BF16)


def dot3(a, b):
    def dot(u, v):
        return jnp.dot(u, v, preferred_element_type=F32)

    return dot(a[0], b[0]) + (dot(a[0], b[1]) + dot(a[1], b[0]))


def kernel(
    panel, cross, diag, out,
    acc, lhi, llo, stage, dbuf, l10, b0, b1, b1_tile, ybuf, yhi, ylo,
    load_sem, stage_sem, out_sem,
    s_ss, s_rs, l_ss, l_rs, pg_ss, pg_rs, yt_ss, yt_rs, yd_ss, yd_rs, cc_ss, cc_rs,
):
    row, col = lax.axis_index("row"), lax.axis_index("col")
    y, core = lax.div(row, 2), lax.rem(row, 2)
    z, x = lax.div(col, 4), lax.rem(col, 4)

    def at(dy=0, dz=0, dx=0, other=False):
        c = 1 - core if other else core
        return (lax.rem(y + dy, 4) * 2 + c, lax.rem(z + dz, 4) * 4 + lax.rem(x + dx, 4))

    def send(src, dst, ss, rs, device):
        return pltpu.make_async_remote_copy(
            src_ref=src, dst_ref=dst, send_sem=ss, recv_sem=rs, device_id=device, device_id_type=MESH
        )

    sent = []

    def go(copy):
        copy.start()
        sent.append(copy)
        return copy

    barrier = pltpu.get_barrier_semaphore()
    partners = [at(dx=i) for i in (1, 2, 3)] + [at(dz=i) for i in (1, 2, 3)]
    partners += [at(dy=i, other=o) for i in range(4) for o in (False, True) if i or o]
    for device in partners:
        pl.semaphore_signal(barrier, inc=1, device_id=device, device_id_type=MESH)

    d_load = pltpu.make_async_copy(diag, dbuf, load_sem.at[0])
    d_load.start()
    l_loads = [
        pltpu.make_async_copy(panel.at[a, 0], stage.at[a % 2], stage_sem.at[a % 2]) for a in range(7)
    ]
    l_loads[0].start()
    l_loads[1].start()
    acc_loads = []
    for q in range(4):
        load = pltpu.make_async_copy(
            cross.at[:, 0, :, pl.ds(256 * q, 256)], acc.at[q], load_sem.at[1 + q]
        )
        load.start()
        acc_loads.append(load)

    def convert(a):
        l_loads[a].wait()
        high, low = split(stage[a % 2])
        lhi[a], llo[a] = high, low
        if a + 2 < 7:
            l_loads[a + 2].start()

    for a in range(3):
        convert(a)
    pl.semaphore_wait(barrier, len(partners))

    def tile_of(r):
        return cross.at[0, 0, :, pl.ds(128 * r, 128)]

    def b0_send(r):
        return send(tile_of(r), b0.at[z, x], s_ss.at[r], s_rs.at[0], (r, col))

    def b1_send(r):
        return send(tile_of(r), b1_tile, s_ss.at[r], s_rs.at[1], (r, col))

    def l10_half(h):
        return panel.at[0, 0, :, pl.ds(1024 * h, 1024)]

    def l10_send(r, h):
        return send(l10_half(h), l10.at[h], l_ss.at[r, h], l_rs.at[h], (r, col))

    l10_parts = [(0, 0), (0, 1)] + [(r, r % 2) for r in range(2, 8)]

    @pl.when(row == 0)
    def _():
        for r in (4, 5, 2, 3, 6, 7, 1):
            b0_send(r).start()
        pltpu.make_async_copy(tile_of(0), b0.at[z, x], s_rs.at[0]).start()

    @pl.when(row == 1)
    def _():
        for r in (4, 5, 2, 3, 6, 7, 0):
            b1_send(r).start()
        pltpu.make_async_copy(tile_of(1), b1_tile, s_rs.at[1]).start()
        for r, h in l10_parts:
            l10_send(r, h).start()
        for h in range(2):
            pltpu.make_async_copy(l10_half(h), l10.at[h], l_rs.at[h]).start()

    for a in range(3, 7):
        convert(a)

    class Gather:
        def __init__(self, number, view, lo, hi):
            self.number, self.view = number, view
            mid = (lo + hi) // 2
            self.first, self.second = pl.ds(lo, mid - lo), pl.ds(mid, hi - mid)

        def copy(self, kind, i, piece, device):
            return send(
                piece, piece, pg_ss.at[self.number, kind, i - 1], pg_rs.at[self.number, kind, i - 1], device
            )

        def phase1(self):
            self.one = []
            for i in (2, 1, 3):
                self.one.append(go(self.copy(0, i, self.view.at[z, x, self.first], at(dx=i))))
                self.one.append(go(self.copy(1, i, self.view.at[z, x, self.second], at(dz=i))))

        def phase2(self):
            for c in self.one:
                c.wait_recv()
            self.two = []
            for i in (2, 1, 3):
                self.two.append(go(self.copy(2, i, self.view.at[z, :, self.first], at(dz=i))))
                self.two.append(go(self.copy(3, i, self.view.at[:, x, self.second], at(dx=i))))

        def done(self):
            for c in self.two:
                c.wait_recv()

    def y_tiles(t):
        copies = {}
        for e in (2, 1, 3):
            rows = pl.ds(0, 128 if e == 2 else NEAR)
            piece = ybuf.at[t, row, z, x, rows]
            copies[e] = go(send(piece, piece, yt_ss.at[t, e - 1], yt_rs.at[t, e - 1], at(dy=e)))
        return copies

    def y_direct(t):
        copies = {}
        for e in (1, 3):
            piece = ybuf.at[t, row, :, :, pl.ds(NEAR, 128 - NEAR)]
            copies[e] = go(send(piece, piece, yd_ss.at[t, e // 2], yd_rs.at[t, e // 2], at(dy=e)))
        return copies

    def slice_of(d):
        return lax.rem(y + d, 4) * 2 + core

    def across(t, d):
        piece = ybuf.at[t, slice_of(d)]
        return go(send(piece, piece, cc_ss.at[t, d], cc_rs.at[t, d], at(other=True)))

    def own_gather(t):
        return Gather(2 + t, ybuf.at[t, row], 0, 128)

    def foreign(t):
        return {
            d: Gather(4 + 3 * t + d - 1, ybuf.at[t, slice_of(d)], 0, 128 if d == 2 else NEAR)
            for d in (2, 1, 3)
        }

    def update(t, d):
        q = lax.rem(y + d, 4)
        for half in range(2):
            high, low = split(ybuf[t, 2 * q + half].reshape(2048, 128))
            yhi[:, 128 * half : 128 * half + 128] = high
            ylo[:, 128 * half : 128 * half + 128] = low

        def body(a, carry):
            ks = slice(2048 * t, 2048 * t + 2048)
            acc[q, a] -= dot3((lhi[a, :, ks], llo[a, :, ks]), (yhi[...], ylo[...]))
            return carry

        lax.fori_loop(0, 7, body, 0)

    d_load.wait()
    send(b0.at[z, x], b0.at[z, x], s_ss.at[0], s_rs.at[0], (row, col)).wait_recv()
    g_b = Gather(0, b0, 0, 128)
    g_b.phase1()
    d0 = split(dbuf[0])
    g_b.phase2()

    l10_across = send(
        l10.at[core], l10.at[core], l_ss.at[1, 0], l_rs.at[core], at(other=True)
    )

    @pl.when(y > 0)
    def _():
        l10_across.wait_recv()
        l10_across.start()

    g_b.done()
    ybuf[0, row, z, x] = dot3(d0, split(b0[...].reshape(2048, 128)))
    own0 = own_gather(0)
    own0.phase1()
    tiles0 = y_tiles(0)
    own0.phase2()

    @pl.when(y > 0)
    def _():
        send(l10.at[core], l10.at[1 - core], l_ss.at[1, 0], l_rs.at[1 - core], at(other=True)).wait_recv()

    @pl.when(y == 0)
    def _():
        for h in range(2):
            send(l10.at[h], l10.at[h], l_ss.at[1, 0], l_rs.at[h], at(other=True)).wait_recv()

    send(b1_tile, b1_tile, s_ss.at[0], s_rs.at[1], (row, col)).wait_recv()
    own0.done()

    mine = ybuf[0, row].reshape(2048, 128)
    b1[z, x] = b1_tile[...] - (
        dot3(split(l10[0]), split(mine[:1024])) + dot3(split(l10[1]), split(mine[1024:]))
    )
    g_f = Gather(1, b1, 0, 128)
    g_f.phase1()
    cross0 = {0: across(0, 0)}
    direct0 = y_direct(0)
    g_f.phase2()
    far0 = foreign(0)
    for d in (2, 1, 3):
        tiles0[4 - d].wait_recv()
        far0[d].phase1()
    for load in acc_loads:
        load.wait()
    cross0[0].wait_recv()
    update(0, 0)
    g_f.done()
    ybuf[1, row, z, x] = dot3(split(dbuf[1]), split(b1[...].reshape(2048, 128)))
    own1 = own_gather(1)
    own1.phase1()
    tiles1 = y_tiles(1)
    for d in (2, 1, 3):
        far0[d].phase2()
    own1.phase2()
    far1 = foreign(1)
    for d in (2, 1, 3):
        tiles1[4 - d].wait_recv()
        far1[d].phase1()
    far0[2].done()
    cross0[2] = across(0, 2)
    for d in (1, 3):
        far0[d].done()
        direct0[4 - d].wait_recv()
        cross0[d] = across(0, d)
    own1.done()
    cross1 = {0: across(1, 0)}
    direct1 = y_direct(1)
    for d in (2, 1, 3):
        far1[d].phase2()
    for d in (2, 1, 3):
        cross0[d].wait_recv()
        update(0, d)

    def store(q):
        return pltpu.make_async_copy(
            acc.at[q], out.at[:, 0, :, pl.ds(pl.multiple_of(256 * q, 256), 256)], out_sem.at[q]
        )

    def finish(d):
        update(1, d)
        q = lax.rem(y + d, 4)

        @pl.when(row < 2)
        def _():
            for half in range(2):
                acc[q, 0, :, 128 * half : 128 * half + 128] = ybuf[row, 2 * q + half, z, x]

        store(q).start()

    cross1[0].wait_recv()
    finish(0)
    far1[2].done()
    cross1[2] = across(1, 2)
    for d in (1, 3):
        far1[d].done()
        direct1[4 - d].wait_recv()
        cross1[d] = across(1, d)
    for d in (2, 1, 3):
        cross1[d].wait_recv()
        finish(d)

    for c in sent:
        c.wait_send()

    @pl.when(row == 0)
    def _():
        for r in range(1, 8):
            b0_send(r).wait_send()

    @pl.when(row == 1)
    def _():
        for r in (0, 2, 3, 4, 5, 6, 7):
            b1_send(r).wait_send()
        for r, h in l10_parts:
            l10_send(r, h).wait_send()

    @pl.when(y > 0)
    def _():
        l10_across.wait_send()

    for q in range(4):
        store(q).wait()


def on_device(lower_panel, test_cross, diag_inverse):
    V = pltpu.VMEM
    return pl.pallas_call(
        kernel,
        out_shape=jax.ShapeDtypeStruct(test_cross.shape, F32),
        in_specs=[pl.BlockSpec(memory_space=pl.ANY)] * 3,
        out_specs=pl.BlockSpec(memory_space=pl.ANY),
        scratch_shapes=[
            V((4, 7, 128, 256), F32),
            V((7, 128, 4096), BF16),
            V((7, 128, 4096), BF16),
            V((2, 128, 4096), F32),
            V((2, 128, 2048), F32),
            V((2, 128, 1024), F32),
            V((4, 4, 128, 128), F32),
            V((4, 4, 128, 128), F32),
            V((128, 128), F32),
            V((2, 8, 4, 4, 128, 128), F32),
            V((2048, 256), BF16),
            V((2048, 256), BF16),
            DMA((5,)), DMA((2,)), DMA((4,)),
            DMA((8,)), DMA((2,)), DMA((8, 2)), DMA((2,)),
            DMA((10, 4, 3)), DMA((10, 4, 3)),
            DMA((2, 3)), DMA((2, 3)), DMA((2, 2)), DMA((2, 2)), DMA((2, 4)), DMA((2, 4)),
        ],
        compiler_params=pltpu.CompilerParams(
            collective_id=0, has_side_effects=True, vmem_limit_bytes=60 * 2**20
        ),
        cost_estimate=pl.CostEstimate(flops=22 * 10**9, bytes_accessed=24 * 10**6, transcendentals=0),
    )(lower_panel, test_cross, diag_inverse)


def solution(mesh):
    placed = (P(None, "row", "col", None), P(None, "row", "col", None), P(None, "col", None))
    return jax.shard_map(
        on_device,
        mesh=mesh,
        in_specs=placed,
        out_specs=P(None, "row", "col", None),
        check_vma=False,
    )
```

```python
import jax
import jax.numpy as jnp
from jax import lax
from jax.experimental import pallas as pl
from jax.experimental.pallas import tpu as pltpu
from jax.sharding import PartitionSpec as P

MESH = pl.DeviceIdType.MESH
DMA = pltpu.SemaphoreType.DMA
F32 = jnp.float32
BF16 = jnp.bfloat16
NEAR = (0, 64)


def split(value):
    high = value.astype(BF16)
    return high, (value - high.astype(F32)).astype(BF16)


def dot3(a, b):
    def dot(u, v):
        return jnp.dot(u, v, preferred_element_type=F32)

    return dot(a[0], b[0]) + (dot(a[0], b[1]) + dot(a[1], b[0]))


def kernel(
    panel, cross, diag, out,
    lhi, llo, stage, dbuf, l10, b0, b1, b1_tile, ybuf, yhi, ylo,
    load_sem, stage_sem,
    s_ss, s_rs, l_ss, l_rs, pg_ss, pg_rs, yt_ss, yt_rs, yd_ss, yd_rs, yr_ss, yr_rs, cc_ss, cc_rs,
):
    row, col = lax.axis_index("row"), lax.axis_index("col")
    y, core = lax.div(row, 2), lax.rem(row, 2)
    z, x = lax.div(col, 4), lax.rem(col, 4)

    def at(dy=0, dz=0, dx=0, other=False):
        c = 1 - core if other else core
        return (lax.rem(y + dy, 4) * 2 + c, lax.rem(z + dz, 4) * 4 + lax.rem(x + dx, 4))

    def send(src, dst, ss, rs, device):
        return pltpu.make_async_remote_copy(
            src_ref=src, dst_ref=dst, send_sem=ss, recv_sem=rs, device_id=device, device_id_type=MESH
        )

    sent = []

    def go(make):
        make().start()
        sent.append(make)
        return make

    barrier = pltpu.get_barrier_semaphore()
    partners = [at(dx=i) for i in (1, 2, 3)] + [at(dz=i) for i in (1, 2, 3)]
    partners += [at(dy=i, other=o) for i in range(4) for o in (False, True) if i or o]
    for device in partners:
        pl.semaphore_signal(barrier, inc=1, device_id=device, device_id_type=MESH)

    d_load = pltpu.make_async_copy(diag, dbuf, load_sem.at[0])
    d_load.start()
    l_loads = [
        pltpu.make_async_copy(panel.at[a, 0], stage.at[a % 2], stage_sem.at[a % 2]) for a in range(7)
    ]
    l_loads[0].start()
    l_loads[1].start()
    out_load = pltpu.make_async_copy(cross, out, load_sem.at[1])
    out_load.start()

    def convert(a):
        l_loads[a].wait()

        def some_rows(g, carry):
            rows = pl.ds(pl.multiple_of(16 * g, 16), 16)
            to = pl.ds(pl.multiple_of(128 * a + 16 * g, 16), 16)
            left = lax.broadcasted_iota(jnp.int32, (16, 128), 1) < 64
            for t in range(2):
                for p in range(8):
                    one = stage[a % 2, rows, 2048 * t + 256 * p : 2048 * t + 256 * p + 128]
                    two = stage[a % 2, rows, 2048 * t + 256 * p + 128 : 2048 * t + 256 * p + 256]
                    parts = (
                        jnp.where(left, one, pltpu.roll(two, 64, 1)),
                        jnp.where(left, pltpu.roll(one, 64, 1), two),
                    )
                    for h in range(2):
                        high, low = split(parts[h])
                        lhi[t, h, to, 128 * p : 128 * p + 128] = high
                        llo[t, h, to, 128 * p : 128 * p + 128] = low
            return carry

        lax.fori_loop(0, 8, some_rows, 0)
        if a + 2 < 7:
            l_loads[a + 2].start()

    for a in range(2):
        convert(a)
    pl.semaphore_wait(barrier, len(partners))

    def tile_of(r):
        return cross.at[pl.ds(0, 128), pl.ds(128 * r, 128)]

    def b0_send(r):
        return send(tile_of(r), b0.at[z, x], s_ss.at[r], s_rs.at[0], (r, col))

    def b1_send(r):
        return send(tile_of(r), b1_tile, s_ss.at[r], s_rs.at[1], (r, col))

    def l10_half(h):
        return panel.at[0, 0, :, pl.ds(1024 * h, 1024)]

    def l10_send(r, h):
        return send(l10_half(h), l10.at[h], l_ss.at[r, h], l_rs.at[h], (r, col))

    l10_parts = [(2, 0), (7, 1), (3, 1), (6, 0), (0, 0), (0, 1)]

    @pl.when(row == 0)
    def _():
        for r in (4, 5, 2, 3, 6, 7, 1):
            b0_send(r).start()
        pltpu.make_async_copy(tile_of(0), b0.at[z, x], s_rs.at[0]).start()

    for a in range(2, 5):
        convert(a)

    @pl.when(row == 1)
    def _():
        for r, h in l10_parts[:4]:
            l10_send(r, h).start()
        for r in (4, 5, 2, 3, 6, 7, 0):
            b1_send(r).start()
        pltpu.make_async_copy(tile_of(1), b1_tile, s_rs.at[1]).start()
        for r, h in l10_parts[4:]:
            l10_send(r, h).start()
        for h in range(2):
            pltpu.make_async_copy(l10_half(h), l10.at[h], l_rs.at[h]).start()

    for a in range(5, 7):
        convert(a)

    class Gather:
        def __init__(self, number, view, lo, hi):
            self.number, self.view = number, view
            mid = (lo + hi) // 2
            self.rows = (lo, mid - lo), (mid, hi - mid)

        def tile(self, half, dz=0, dx=0):
            return self.view.at[lax.rem(z + dz, 4), lax.rem(x + dx, 4), pl.ds(*self.rows[half])]

        def line(self, half):
            if half == 0:
                return self.view.at[z, :, pl.ds(*self.rows[half])]
            return self.view.at[:, x, pl.ds(*self.rows[half])]

        def copy(self, kind, i, piece, part=0):
            device = at(dx=i) if kind in (0, 3) else at(dz=i)
            ss, rs = pg_ss.at[self.number, kind, i - 1, part], pg_rs.at[self.number, kind, i - 1]
            return send(piece, piece, ss, rs, device)

        def phase1(self):
            self.one = {}
            for i in (2, 1, 3):
                for half in range(2):
                    self.one[half, i] = go(lambda half=half, i=i: self.copy(half, i, self.tile(half)))

        def phase2(self):
            for half, i in self.one:
                self.one[half, i]().wait_recv()
            for i in (2, 1, 3):
                for half in range(2):
                    go(lambda half=half, i=i: self.copy(2 + half, i, self.line(half)))

        def own(self):
            self.phase1()
            for i in (2, 1, 3):
                for half in range(2):
                    go(lambda half=half, i=i: self.copy(2 + half, i, self.tile(half)))

        def forward(self):
            for k, i in enumerate((1, 3, 2)):
                for half in range(2):
                    self.one[half, i]().wait_recv()
                    back = {"dx": 4 - i} if half == 0 else {"dz": 4 - i}
                    for to in (2, 1, 3):
                        go(
                            lambda half=half, to=to, back=back, k=k: self.copy(
                                2 + half, to, self.tile(half, **back), 1 + k
                            )
                        )

        def done(self, halves=(0, 1), peers=(1, 3, 2)):
            for half in halves:
                for i in peers:
                    self.copy(2 + half, i, self.line(half)).wait_recv()

    def slice_of(d):
        return lax.rem(y + d, 4) * 2 + core

    def y_tiles(t):
        copies = {}
        for e in (2, 1, 3):
            rows = 128 if e == 2 else NEAR[t]
            if not rows:
                continue

            def make(e=e, rows=rows):
                piece = ybuf.at[t, row, z, x, pl.ds(0, rows)]
                return send(piece, piece, yt_ss.at[t, e - 1], yt_rs.at[t, e - 1], at(dy=e))

            copies[e] = go(make)
        return copies

    def y_line(t, back):
        for e in (1, 3):

            def make(e=e):
                piece = ybuf.at[t, row, :, lax.rem(x + 4 - back, 4), pl.ds(64, 64)]
                return send(piece, piece, yd_ss.at[t, e // 2, back], yd_rs.at[t, e // 2], at(dy=e))

            go(make)

    def y_line_wait(t, e):
        piece = ybuf.at[t, row, :, :, pl.ds(64, 64)]
        send(piece, piece, yd_ss.at[t, e // 2, 0], yd_rs.at[t, e // 2], at(dy=e)).wait_recv()

    def y_rest(t):
        copies = {}
        if NEAR[t] < 64:
            for e in (1, 3):

                def make(e=e):
                    piece = ybuf.at[t, row, :, :, pl.ds(NEAR[t], 64 - NEAR[t])]
                    return send(piece, piece, yr_ss.at[t, e // 2], yr_rs.at[t, e // 2], at(dy=e))

                copies[e] = go(make)
        return copies

    def across_copy(t, d, h):
        piece = ybuf.at[t, slice_of(d), :, :, pl.ds(64 * h, 64)]
        return send(piece, piece, cc_ss.at[t, d, h], cc_rs.at[t, d, h], at(other=True))

    def across(t, d, h):
        go(lambda: across_copy(t, d, h))

    def crossed(t, d, h):
        across_copy(t, d, h).wait_recv()

    def own_lines(t, gather, peers):
        for i in peers:
            gather.done((1,), (i,))
            y_line(t, i)

    own = [Gather(2 + t, ybuf.at[t, row], 0, 128) for t in range(2)]
    far = [
        {
            d: Gather(4 + 3 * t + d - 1, ybuf.at[t, slice_of(d)], 0, 128 if d == 2 else NEAR[t])
            for d in (2, 1, 3)
            if d == 2 or NEAR[t]
        }
        for t in range(2)
    ]
    g_b, g_f = Gather(0, b0, 0, 128), Gather(1, b1, 0, 128)

    def arrived(t, d, h):
        if d == 2:
            far[t][2].done((h,))
        elif h == 1:
            y_line_wait(t, 4 - d)
        else:
            if d in far[t]:
                far[t][d].done()
            if NEAR[t] < 64:
                rest[t][4 - d]().wait_recv()
        across(t, d, h)

    d_load.wait()
    b0_send(0).wait_recv()
    g_b.own()
    g_b.forward()
    d0 = split(dbuf[0])
    g_b.done()
    ybuf[0, row, z, x] = dot3(d0, split(b0[...].reshape(2048, 128)))
    own[0].own()
    tiles0 = y_tiles(0)

    half = l10.at[core]
    l10_on = send(half, half, l_ss.at[1, 1], l_rs.at[core], (4 + core, col))
    l10_across = send(half, half, l_ss.at[1, 0], l_rs.at[core], at(other=True))
    first = jnp.logical_or(row == 2, row == 7)

    @pl.when(first)
    def _():
        l10_on.wait_recv()
        l10_on.start()
        l10_across.start()

    own[0].forward()
    y_line(0, 0)

    @pl.when(jnp.logical_and(y > 0, jnp.logical_not(first)))
    def _():
        l10_across.wait_recv()
        l10_across.start()

    @pl.when(y > 0)
    def _():
        send(half, l10.at[1 - core], l_ss.at[1, 0], l_rs.at[1 - core], at(other=True)).wait_recv()

    @pl.when(y == 0)
    def _():
        for h in range(2):
            send(l10.at[h], l10.at[h], l_ss.at[1, 0], l_rs.at[h], at(other=True)).wait_recv()

    send(b1_tile, b1_tile, s_ss.at[0], s_rs.at[1], (row, col)).wait_recv()
    lower = [split(l10[h]) for h in range(2)]
    own_lines(0, own[0], (1, 3))
    own_lines(0, own[0], (2,))
    own[0].done((0,))

    mine = ybuf[0, row].reshape(2048, 128)
    b1[z, x] = b1_tile[...] - (dot3(lower[0], split(mine[:1024])) + dot3(lower[1], split(mine[1024:])))
    g_f.own()
    across(0, 0, 0)
    across(0, 0, 1)
    rest = [y_rest(0), {}]
    tiles0[2]().wait_recv()
    far[0][2].own()
    g_f.forward()
    far[0][2].forward()
    out_load.wait()

    def solve_second():
        arrived(0, 1, 1)
        arrived(0, 3, 1)
        d1 = split(dbuf[1])
        g_f.done()
        ybuf[1, row, z, x] = dot3(d1, split(b1[...].reshape(2048, 128)))
        own[1].own()
        second_tiles.update(y_tiles(1))
        crossed(0, 1, 1)

    second_tiles = {}

    def start_far():
        own[1].forward()
        y_line(1, 0)
        second_tiles[2]().wait_recv()
        far[1][2].own()
        for d in (1, 3):
            second_tiles[4 - d]().wait_recv()
            far[1][d].phase1()
        arrived(0, 2, 0)
        arrived(0, 2, 1)
        crossed(0, 2, 0)

    def forward_far():
        own_lines(1, own[1], (1, 3))
        far[1][2].forward()
        crossed(0, 2, 1)

    def second_gathered():
        own_lines(1, own[1], (2,))
        own[1].done((0,))
        across(1, 0, 0)
        across(1, 0, 1)
        far[1][1].phase2()
        far[1][3].phase2()
        arrived(0, 1, 0)
        arrived(0, 3, 0)
        crossed(0, 1, 0)

    def opposite():
        arrived(1, 2, 0)
        arrived(1, 2, 1)
        crossed(1, 0, 1)

    def near_high():
        arrived(1, 1, 1)
        arrived(1, 3, 1)
        crossed(1, 2, 1)

    def near_low():
        arrived(1, 1, 0)
        arrived(1, 3, 0)
        crossed(1, 1, 1)

    order = [(0, 0, 0), (0, 0, 1), (0, 1, 1), (0, 3, 1), (0, 2, 0), (0, 2, 1), (0, 1, 0), (0, 3, 0)]
    order += [(1, 0, 0), (1, 0, 1), (1, 2, 0), (1, 2, 1), (1, 1, 1), (1, 3, 1), (1, 1, 0), (1, 3, 0)]
    controls = {
        (0, 1, 1): solve_second,
        (0, 2, 0): start_far,
        (0, 2, 1): forward_far,
        (0, 1, 0): second_gathered,
        (1, 0, 1): opposite,
        (1, 2, 1): near_high,
        (1, 1, 1): near_low,
    }

    def job(k, carry):
        for i, unit in enumerate(order):
            pl.when(k == i)(controls.get(unit, lambda unit=unit: crossed(*unit)))

        def of(place):
            return sum((k == i).astype(jnp.int32) * unit[place] for i, unit in enumerate(order) if unit[place])

        t, d, h = of(0), of(1), of(2)
        q = lax.rem(y + d, 4)
        columns = pl.ds(pl.multiple_of(256 * q, 256), 256)
        for c in range(2):
            rows = ybuf[t, 2 * q + c, :, :, pl.ds(pl.multiple_of(64 * h, 64), 64), :]
            high, low = split(rows.reshape(1024, 128))
            yhi[:, 128 * c : 128 * c + 128] = high
            ylo[:, 128 * c : 128 * c + 128] = low
        out[:, columns] -= dot3((lhi[t, h], llo[t, h]), (yhi[...], ylo[...]))

        return carry

    lax.fori_loop(0, 16, job, 0)

    @pl.when(row < 2)
    def _():
        for r in range(8):
            out[0:128, 128 * r : 128 * r + 128] = ybuf[row, r, z, x]

    for make in sent:
        make().wait_send()

    @pl.when(row == 0)
    def _():
        for r in range(1, 8):
            b0_send(r).wait_send()

    @pl.when(row == 1)
    def _():
        for r in (0, 2, 3, 4, 5, 6, 7):
            b1_send(r).wait_send()
        for r, h in l10_parts:
            l10_send(r, h).wait_send()

    @pl.when(y > 0)
    def _():
        l10_across.wait_send()

    @pl.when(first)
    def _():
        l10_on.wait_send()


def on_device(lower_panel, test_cross, diag_inverse):
    V = pltpu.VMEM
    out = pl.pallas_call(
        kernel,
        out_shape=pltpu.VMEM((896, 1024), F32),
        in_specs=[pl.BlockSpec(memory_space=pl.ANY)] * 3,
        out_specs=pl.BlockSpec(memory_space=pltpu.VMEM),
        scratch_shapes=[
            V((2, 2, 896, 1024), BF16),
            V((2, 2, 896, 1024), BF16),
            V((2, 128, 4096), F32),
            V((2, 128, 2048), F32),
            V((2, 128, 1024), F32),
            V((4, 4, 128, 128), F32),
            V((4, 4, 128, 128), F32),
            V((128, 128), F32),
            V((2, 8, 4, 4, 128, 128), F32),
            V((1024, 256), BF16),
            V((1024, 256), BF16),
            DMA((2,)), DMA((2,)),
            DMA((8,)), DMA((2,)), DMA((8, 2)), DMA((2,)),
            DMA((10, 4, 3, 4)), DMA((10, 4, 3)),
            DMA((2, 3)), DMA((2, 3)), DMA((2, 2, 4)), DMA((2, 2)), DMA((2, 2)), DMA((2, 2)),
            DMA((2, 4, 2)), DMA((2, 4, 2)),
        ],
        compiler_params=pltpu.CompilerParams(
            collective_id=0, has_side_effects=True, vmem_limit_bytes=54 * 2**20
        ),
        cost_estimate=pl.CostEstimate(flops=22 * 10**9, bytes_accessed=24 * 10**6, transcendentals=0),
    )(lower_panel, test_cross.reshape(896, 1024), diag_inverse)
    return out.reshape(test_cross.shape)


def solution(mesh):
    placed = (P(None, "row", "col", None), P(None, "row", "col", None), P(None, "col", None))
    return jax.shard_map(
        on_device,
        mesh=mesh,
        in_specs=placed,
        out_specs=P(None, "row", "col", None),
        check_vma=False,
    )
```

```python
import jax
import jax.numpy as jnp
from jax import lax
from jax.experimental import pallas as pl
from jax.experimental.pallas import tpu as pltpu
from jax.sharding import PartitionSpec as P

MESH = pl.DeviceIdType.MESH
DMA = pltpu.SemaphoreType.DMA
F32 = jnp.float32
BF16 = jnp.bfloat16
NEAR = (0, 64)


def split(value):
    high = value.astype(BF16)
    return high, (value - high.astype(F32)).astype(BF16)


def dot3(a, b):
    def dot(u, v):
        return jnp.dot(u, v, preferred_element_type=F32)

    return dot(a[0], b[0]) + (dot(a[0], b[1]) + dot(a[1], b[0]))


def kernel(
    panel, cross, diag, out,
    lhi, llo, stage, dbuf, l10, b0, b1, b1_tile, ybuf, yhi, ylo,
    load_sem, stage_sem,
    s_ss, s_rs, l_ss, l_rs, pg_ss, pg_rs, yt_ss, yt_rs, yd_ss, yd_rs, yr_ss, yr_rs, cc_ss, cc_rs,
):
    row, col = lax.axis_index("row"), lax.axis_index("col")
    y, core = lax.div(row, 2), lax.rem(row, 2)
    z, x = lax.div(col, 4), lax.rem(col, 4)

    def at(dy=0, dz=0, dx=0, other=False):
        c = 1 - core if other else core
        return (lax.rem(y + dy, 4) * 2 + c, lax.rem(z + dz, 4) * 4 + lax.rem(x + dx, 4))

    def send(src, dst, ss, rs, device):
        return pltpu.make_async_remote_copy(
            src_ref=src, dst_ref=dst, send_sem=ss, recv_sem=rs, device_id=device, device_id_type=MESH
        )

    sent = []

    def go(make):
        make().start()
        sent.append(make)
        return make

    barrier = pltpu.get_barrier_semaphore()
    partners = [at(dx=i) for i in (1, 2, 3)] + [at(dz=i) for i in (1, 2, 3)]
    partners += [at(dy=i, other=o) for i in range(4) for o in (False, True) if i or o]
    for device in partners:
        pl.semaphore_signal(barrier, inc=1, device_id=device, device_id_type=MESH)

    d_load = pltpu.make_async_copy(diag, dbuf, load_sem.at[0])
    d_load.start()
    l_loads = [
        pltpu.make_async_copy(panel.at[a, 0], stage.at[a % 2], stage_sem.at[a % 2]) for a in range(7)
    ]
    l_loads[0].start()
    l_loads[1].start()
    out_load = pltpu.make_async_copy(cross, out, load_sem.at[1])
    out_load.start()

    def convert(a):
        l_loads[a].wait()

        def some_rows(g, carry):
            rows = pl.ds(pl.multiple_of(16 * g, 16), 16)
            to = pl.ds(pl.multiple_of(128 * a + 16 * g, 16), 16)
            left = lax.broadcasted_iota(jnp.int32, (16, 128), 1) < 64
            for t in range(2):
                for p in range(8):
                    one = stage[a % 2, rows, 2048 * t + 256 * p : 2048 * t + 256 * p + 128]
                    two = stage[a % 2, rows, 2048 * t + 256 * p + 128 : 2048 * t + 256 * p + 256]
                    parts = (
                        jnp.where(left, one, pltpu.roll(two, 64, 1)),
                        jnp.where(left, pltpu.roll(one, 64, 1), two),
                    )
                    for h in range(2):
                        high, low = split(parts[h])
                        lhi[t, h, to, 128 * p : 128 * p + 128] = high
                        llo[t, h, to, 128 * p : 128 * p + 128] = low
            return carry

        lax.fori_loop(0, 8, some_rows, 0)
        if a + 2 < 7:
            l_loads[a + 2].start()

    for a in range(2):
        convert(a)
    pl.semaphore_wait(barrier, len(partners))

    def tile_of(r):
        return cross.at[pl.ds(0, 128), pl.ds(128 * r, 128)]

    def b0_send(r):
        return send(tile_of(r), b0.at[z, x], s_ss.at[r], s_rs.at[0], (r, col))

    def b1_send(r):
        return send(tile_of(r), b1_tile, s_ss.at[r], s_rs.at[1], (r, col))

    def l10_half(h):
        return panel.at[0, 0, :, pl.ds(1024 * h, 1024)]

    def l10_send(r, h):
        return send(l10_half(h), l10.at[h], l_ss.at[r, h], l_rs.at[h], (r, col))

    l10_parts = [(2, 0), (7, 1), (3, 1), (6, 0), (0, 0), (0, 1)]

    @pl.when(row == 0)
    def _():
        for r in (4, 5, 2, 3, 6, 7, 1):
            b0_send(r).start()
        pltpu.make_async_copy(tile_of(0), b0.at[z, x], s_rs.at[0]).start()

    for a in range(2, 5):
        convert(a)

    @pl.when(row == 1)
    def _():
        for r, h in l10_parts[:2]:
            l10_send(r, h).start()
        for r in (4, 5, 2, 3, 6, 7, 0):
            b1_send(r).start()
        pltpu.make_async_copy(tile_of(1), b1_tile, s_rs.at[1]).start()
        for h in range(2):
            pltpu.make_async_copy(l10_half(h), l10.at[h], l_rs.at[h]).start()

    for a in range(5, 7):
        convert(a)

    class Gather:
        def __init__(self, number, view, lo, hi):
            self.number, self.view = number, view
            mid = (lo + hi) // 2
            self.rows = (lo, mid - lo), (mid, hi - mid)

        def tile(self, half, dz=0, dx=0):
            return self.view.at[lax.rem(z + dz, 4), lax.rem(x + dx, 4), pl.ds(*self.rows[half])]

        def line(self, half):
            if half == 0:
                return self.view.at[z, :, pl.ds(*self.rows[half])]
            return self.view.at[:, x, pl.ds(*self.rows[half])]

        def copy(self, kind, i, piece, part=0):
            device = at(dx=i) if kind in (0, 3) else at(dz=i)
            ss, rs = pg_ss.at[self.number, kind, i - 1, part], pg_rs.at[self.number, kind, i - 1]
            return send(piece, piece, ss, rs, device)

        def phase1(self):
            self.one = {}
            for i in (2, 1, 3):
                for half in range(2):
                    self.one[half, i] = go(lambda half=half, i=i: self.copy(half, i, self.tile(half)))

        def phase2(self):
            for half, i in self.one:
                self.one[half, i]().wait_recv()
            for i in (2, 1, 3):
                for half in range(2):
                    go(lambda half=half, i=i: self.copy(2 + half, i, self.line(half)))

        def own(self):
            self.phase1()
            for i in (2, 1, 3):
                for half in range(2):
                    go(lambda half=half, i=i: self.copy(2 + half, i, self.tile(half)))

        def forward(self):
            for k, i in enumerate((1, 3, 2)):
                for half in range(2):
                    self.one[half, i]().wait_recv()
                    back = {"dx": 4 - i} if half == 0 else {"dz": 4 - i}
                    for to in (2, 1, 3):
                        go(
                            lambda half=half, to=to, back=back, k=k: self.copy(
                                2 + half, to, self.tile(half, **back), 1 + k
                            )
                        )

        def done(self, halves=(0, 1), peers=(1, 3, 2)):
            for half in halves:
                for i in peers:
                    self.copy(2 + half, i, self.line(half)).wait_recv()

    def slice_of(d):
        return lax.rem(y + d, 4) * 2 + core

    def y_tiles(t):
        copies = {}
        for e in (2, 1, 3):
            rows = 128 if e == 2 else NEAR[t]
            if not rows:
                continue

            def make(e=e, rows=rows):
                piece = ybuf.at[t, row, z, x, pl.ds(0, rows)]
                return send(piece, piece, yt_ss.at[t, e - 1], yt_rs.at[t, e - 1], at(dy=e))

            copies[e] = go(make)
        return copies

    def y_line(t, back):
        for e in (1, 3):

            def make(e=e):
                piece = ybuf.at[t, row, :, lax.rem(x + 4 - back, 4), pl.ds(64, 64)]
                return send(piece, piece, yd_ss.at[t, e // 2, back], yd_rs.at[t, e // 2], at(dy=e))

            go(make)

    def y_line_wait(t, e):
        piece = ybuf.at[t, row, :, :, pl.ds(64, 64)]
        send(piece, piece, yd_ss.at[t, e // 2, 0], yd_rs.at[t, e // 2], at(dy=e)).wait_recv()

    def y_rest(t):
        copies = {}
        if NEAR[t] < 64:
            for e in (1, 3):

                def make(e=e):
                    piece = ybuf.at[t, row, :, :, pl.ds(NEAR[t], 64 - NEAR[t])]
                    return send(piece, piece, yr_ss.at[t, e // 2], yr_rs.at[t, e // 2], at(dy=e))

                copies[e] = go(make)
        return copies

    def across_copy(t, d, h):
        piece = ybuf.at[t, slice_of(d), :, :, pl.ds(64 * h, 64)]
        return send(piece, piece, cc_ss.at[t, d, h], cc_rs.at[t, d, h], at(other=True))

    def across(t, d, h):
        go(lambda: across_copy(t, d, h))

    def crossed(t, d, h):
        across_copy(t, d, h).wait_recv()

    def own_lines(t, gather, peers):
        for i in peers:
            gather.done((1,), (i,))
            y_line(t, i)

    own = [Gather(2 + t, ybuf.at[t, row], 0, 128) for t in range(2)]
    far = [
        {
            d: Gather(4 + 3 * t + d - 1, ybuf.at[t, slice_of(d)], 0, 128 if d == 2 else NEAR[t])
            for d in (2, 1, 3)
            if d == 2 or NEAR[t]
        }
        for t in range(2)
    ]
    g_b, g_f = Gather(0, b0, 0, 128), Gather(1, b1, 0, 128)

    def arrived(t, d, h):
        if d == 2:
            far[t][2].done((h,))
        elif h == 1:
            y_line_wait(t, 4 - d)
        else:
            if d in far[t]:
                far[t][d].done()
            if NEAR[t] < 64:
                rest[t][4 - d]().wait_recv()
        across(t, d, h)

    d_load.wait()
    b0_send(0).wait_recv()
    g_b.own()
    g_b.forward()

    @pl.when(row == 1)
    def _():
        for r, h in l10_parts[:2]:
            l10_send(r, h).wait_send()
        for r, h in l10_parts[2:]:
            l10_send(r, h).start()

    d0 = split(dbuf[0])

    half = l10.at[core]
    l10_on = send(half, half, l_ss.at[1, 1], l_rs.at[core], (4 + core, col))
    l10_across = send(half, half, l_ss.at[1, 0], l_rs.at[core], at(other=True))
    first = jnp.logical_or(row == 2, row == 7)

    @pl.when(first)
    def _():
        l10_on.wait_recv()
        l10_on.start()
        l10_across.start()

    g_b.done()
    ybuf[0, row, z, x] = dot3(d0, split(b0[...].reshape(2048, 128)))
    own[0].own()
    tiles0 = y_tiles(0)

    own[0].forward()
    y_line(0, 0)

    own_lines(0, own[0], (1, 3))
    @pl.when(jnp.logical_and(y > 0, jnp.logical_not(first)))
    def _():
        l10_across.wait_recv()
        l10_across.start()

    @pl.when(y > 0)
    def _():
        send(half, l10.at[1 - core], l_ss.at[1, 0], l_rs.at[1 - core], at(other=True)).wait_recv()

    @pl.when(y == 0)
    def _():
        for h in range(2):
            send(l10.at[h], l10.at[h], l_ss.at[1, 0], l_rs.at[h], at(other=True)).wait_recv()

    send(b1_tile, b1_tile, s_ss.at[0], s_rs.at[1], (row, col)).wait_recv()
    lower = [split(l10[h]) for h in range(2)]
    own_lines(0, own[0], (2,))
    own[0].done((0,))

    mine = ybuf[0, row].reshape(2048, 128)
    b1[z, x] = b1_tile[...] - (dot3(lower[0], split(mine[:1024])) + dot3(lower[1], split(mine[1024:])))
    g_f.own()
    across(0, 0, 0)
    across(0, 0, 1)
    rest = [y_rest(0), {}]
    tiles0[2]().wait_recv()
    far[0][2].own()
    g_f.forward()
    far[0][2].forward()
    out_load.wait()

    def solve_second():
        arrived(0, 1, 1)
        arrived(0, 3, 1)
        d1 = split(dbuf[1])
        g_f.done()
        ybuf[1, row, z, x] = dot3(d1, split(b1[...].reshape(2048, 128)))
        own[1].own()
        second_tiles.update(y_tiles(1))
        crossed(0, 1, 1)

    second_tiles = {}

    def start_far():
        own[1].forward()
        y_line(1, 0)
        second_tiles[2]().wait_recv()
        far[1][2].own()
        for d in (1, 3):
            second_tiles[4 - d]().wait_recv()
            far[1][d].phase1()
        arrived(0, 2, 0)
        arrived(0, 2, 1)
        crossed(0, 2, 0)

    def forward_far():
        own_lines(1, own[1], (1, 3))
        far[1][2].forward()
        crossed(0, 2, 1)

    def second_gathered():
        own_lines(1, own[1], (2,))
        own[1].done((0,))
        across(1, 0, 0)
        across(1, 0, 1)
        far[1][1].phase2()
        far[1][3].phase2()
        arrived(0, 1, 0)
        arrived(0, 3, 0)
        crossed(0, 1, 0)

    def opposite():
        arrived(1, 2, 0)
        arrived(1, 2, 1)
        crossed(1, 0, 1)

    def near_high():
        arrived(1, 1, 1)
        arrived(1, 3, 1)
        crossed(1, 2, 1)

    def near_low():
        arrived(1, 1, 0)
        arrived(1, 3, 0)
        crossed(1, 1, 1)

    order = [(0, 0, 0), (0, 0, 1), (0, 1, 1), (0, 3, 1), (0, 2, 0), (0, 2, 1), (0, 1, 0), (0, 3, 0)]
    order += [(1, 0, 0), (1, 0, 1), (1, 2, 0), (1, 2, 1), (1, 1, 1), (1, 3, 1), (1, 1, 0), (1, 3, 0)]
    controls = {
        (0, 1, 1): solve_second,
        (0, 2, 0): start_far,
        (0, 2, 1): forward_far,
        (0, 1, 0): second_gathered,
        (1, 0, 1): opposite,
        (1, 2, 1): near_high,
        (1, 1, 1): near_low,
    }

    def job(k, carry):
        for i, unit in enumerate(order):
            pl.when(k == i)(controls.get(unit, lambda unit=unit: crossed(*unit)))

        def of(place):
            return sum((k == i).astype(jnp.int32) * unit[place] for i, unit in enumerate(order) if unit[place])

        t, d, h = of(0), of(1), of(2)
        q = lax.rem(y + d, 4)
        columns = pl.ds(pl.multiple_of(256 * q, 256), 256)
        for c in range(2):
            rows = ybuf[t, 2 * q + c, :, :, pl.ds(pl.multiple_of(64 * h, 64), 64), :]
            high, low = split(rows.reshape(1024, 128))
            yhi[:, 128 * c : 128 * c + 128] = high
            ylo[:, 128 * c : 128 * c + 128] = low
        out[:, columns] -= dot3((lhi[t, h], llo[t, h]), (yhi[...], ylo[...]))

        return carry

    lax.fori_loop(0, 16, job, 0)

    @pl.when(row < 2)
    def _():
        for r in range(8):
            out[0:128, 128 * r : 128 * r + 128] = ybuf[row, r, z, x]

    for make in sent:
        make().wait_send()

    @pl.when(row == 0)
    def _():
        for r in range(1, 8):
            b0_send(r).wait_send()

    @pl.when(row == 1)
    def _():
        for r in (0, 2, 3, 4, 5, 6, 7):
            b1_send(r).wait_send()
        for r, h in l10_parts[2:]:
            l10_send(r, h).wait_send()

    @pl.when(y > 0)
    def _():
        l10_across.wait_send()

    @pl.when(first)
    def _():
        l10_on.wait_send()


def on_device(lower_panel, test_cross, diag_inverse):
    V = pltpu.VMEM
    out = pl.pallas_call(
        kernel,
        out_shape=pltpu.VMEM((896, 1024), F32),
        in_specs=[pl.BlockSpec(memory_space=pl.ANY)] * 3,
        out_specs=pl.BlockSpec(memory_space=pltpu.VMEM),
        scratch_shapes=[
            V((2, 2, 896, 1024), BF16),
            V((2, 2, 896, 1024), BF16),
            V((2, 128, 4096), F32),
            V((2, 128, 2048), F32),
            V((2, 128, 1024), F32),
            V((4, 4, 128, 128), F32),
            V((4, 4, 128, 128), F32),
            V((128, 128), F32),
            V((2, 8, 4, 4, 128, 128), F32),
            V((1024, 256), BF16),
            V((1024, 256), BF16),
            DMA((2,)), DMA((2,)),
            DMA((8,)), DMA((2,)), DMA((8, 2)), DMA((2,)),
            DMA((10, 4, 3, 4)), DMA((10, 4, 3)),
            DMA((2, 3)), DMA((2, 3)), DMA((2, 2, 4)), DMA((2, 2)), DMA((2, 2)), DMA((2, 2)),
            DMA((2, 4, 2)), DMA((2, 4, 2)),
        ],
        compiler_params=pltpu.CompilerParams(
            collective_id=0, has_side_effects=True, vmem_limit_bytes=54 * 2**20
        ),
        cost_estimate=pl.CostEstimate(flops=22 * 10**9, bytes_accessed=24 * 10**6, transcendentals=0),
    )(lower_panel, test_cross.reshape(896, 1024), diag_inverse)
    return out.reshape(test_cross.shape)


def solution(mesh):
    placed = (P(None, "row", "col", None), P(None, "row", "col", None), P(None, "col", None))
    return jax.shard_map(
        on_device,
        mesh=mesh,
        in_specs=placed,
        out_specs=P(None, "row", "col", None),
        check_vma=False,
    )
```

```python
import jax
import jax.numpy as jnp
from jax import lax
from jax.experimental import pallas as pl
from jax.experimental.pallas import tpu as pltpu
from jax.sharding import PartitionSpec as P

MESH = pl.DeviceIdType.MESH
DMA = pltpu.SemaphoreType.DMA
F32 = jnp.float32
BF16 = jnp.bfloat16
NEAR = (0, 64)


def split(value):
    high = value.astype(BF16)
    return high, (value - high.astype(F32)).astype(BF16)


def dot3(a, b):
    def dot(u, v):
        return jnp.dot(u, v, preferred_element_type=F32)

    return dot(a[0], b[0]) + (dot(a[0], b[1]) + dot(a[1], b[0]))


def kernel(
    panel, cross, diag, out,
    lhi, llo, stage, dbuf, l10, b0, b1, b1_tile, ybuf, yhi, ylo,
    load_sem, stage_sem,
    s_ss, s_rs, l_ss, l_rs, pg_ss, pg_rs, yt_ss, yt_rs, yd_ss, yd_rs, yr_ss, yr_rs, cc_ss, cc_rs,
):
    row, col = lax.axis_index("row"), lax.axis_index("col")
    y, core = lax.div(row, 2), lax.rem(row, 2)
    z, x = lax.div(col, 4), lax.rem(col, 4)

    def at(dy=0, dz=0, dx=0, other=False):
        c = 1 - core if other else core
        return (lax.rem(y + dy, 4) * 2 + c, lax.rem(z + dz, 4) * 4 + lax.rem(x + dx, 4))

    def send(src, dst, ss, rs, device):
        return pltpu.make_async_remote_copy(
            src_ref=src, dst_ref=dst, send_sem=ss, recv_sem=rs, device_id=device, device_id_type=MESH
        )

    sent = []

    def go(make):
        make().start()
        sent.append(make)
        return make

    barrier = pltpu.get_barrier_semaphore()
    partners = [at(dx=i) for i in (1, 2, 3)] + [at(dz=i) for i in (1, 2, 3)]
    partners += [at(dy=i, other=o) for i in range(4) for o in (False, True) if i or o]
    for device in partners:
        pl.semaphore_signal(barrier, inc=1, device_id=device, device_id_type=MESH)

    d_load = pltpu.make_async_copy(diag, dbuf, load_sem.at[0])
    d_load.start()
    l_loads = [
        pltpu.make_async_copy(panel.at[a, 0], stage.at[a % 2], stage_sem.at[a % 2]) for a in range(7)
    ]
    l_loads[0].start()
    l_loads[1].start()
    out_load = pltpu.make_async_copy(cross, out, load_sem.at[1])
    out_load.start()

    def convert(a):
        l_loads[a].wait()

        def some_rows(g, carry):
            rows = pl.ds(pl.multiple_of(16 * g, 16), 16)
            to = pl.ds(pl.multiple_of(128 * a + 16 * g, 16), 16)
            left = lax.broadcasted_iota(jnp.int32, (16, 128), 1) < 64
            for t in range(2):
                for p in range(8):
                    one = stage[a % 2, rows, 2048 * t + 256 * p : 2048 * t + 256 * p + 128]
                    two = stage[a % 2, rows, 2048 * t + 256 * p + 128 : 2048 * t + 256 * p + 256]
                    parts = (
                        jnp.where(left, one, pltpu.roll(two, 64, 1)),
                        jnp.where(left, pltpu.roll(one, 64, 1), two),
                    )
                    for h in range(2):
                        high, low = split(parts[h])
                        lhi[t, h, to, 128 * p : 128 * p + 128] = high
                        llo[t, h, to, 128 * p : 128 * p + 128] = low
            return carry

        lax.fori_loop(0, 8, some_rows, 0)
        if a + 2 < 7:
            l_loads[a + 2].start()

    for a in range(2):
        convert(a)
    pl.semaphore_wait(barrier, len(partners))

    def tile_of(r):
        return cross.at[pl.ds(0, 128), pl.ds(128 * r, 128)]

    def b0_send(r):
        return send(tile_of(r), b0.at[z, x], s_ss.at[r], s_rs.at[0], (r, col))

    def b1_send(r):
        return send(tile_of(r), b1_tile, s_ss.at[r], s_rs.at[1], (r, col))

    def l10_half(h):
        return panel.at[0, 0, :, pl.ds(1024 * h, 1024)]

    def l10_send(r, h):
        return send(l10_half(h), l10.at[h], l_ss.at[r, h], l_rs.at[h], (r, col))

    l10_parts = [(2, 0), (7, 1), (3, 1), (6, 0), (0, 0), (0, 1)]

    @pl.when(row == 0)
    def _():
        for r in (4, 5, 2, 3, 6, 7, 1):
            b0_send(r).start()
        pltpu.make_async_copy(tile_of(0), b0.at[z, x], s_rs.at[0]).start()

    for a in range(2, 5):
        convert(a)

    @pl.when(row == 1)
    def _():
        for r, h in l10_parts[:2]:
            l10_send(r, h).start()
        for r in (4, 5, 2, 3, 6, 7, 0):
            b1_send(r).start()
        pltpu.make_async_copy(tile_of(1), b1_tile, s_rs.at[1]).start()
        for h in range(2):
            pltpu.make_async_copy(l10_half(h), l10.at[h], l_rs.at[h]).start()

    class Gather:
        def __init__(self, number, view, lo, hi):
            self.number, self.view = number, view
            mid = (lo + hi) // 2
            self.rows = (lo, mid - lo), (mid, hi - mid)

        def tile(self, half, dz=0, dx=0):
            return self.view.at[lax.rem(z + dz, 4), lax.rem(x + dx, 4), pl.ds(*self.rows[half])]

        def line(self, half):
            if half == 0:
                return self.view.at[z, :, pl.ds(*self.rows[half])]
            return self.view.at[:, x, pl.ds(*self.rows[half])]

        def copy(self, kind, i, piece, part=0):
            device = at(dx=i) if kind in (0, 3) else at(dz=i)
            ss, rs = pg_ss.at[self.number, kind, i - 1, part], pg_rs.at[self.number, kind, i - 1]
            return send(piece, piece, ss, rs, device)

        def phase1(self):
            self.one = {}
            for i in (2, 1, 3):
                for half in range(2):
                    self.one[half, i] = go(lambda half=half, i=i: self.copy(half, i, self.tile(half)))

        def phase2(self):
            for half, i in self.one:
                self.one[half, i]().wait_recv()
            for i in (2, 1, 3):
                for half in range(2):
                    go(lambda half=half, i=i: self.copy(2 + half, i, self.line(half)))

        def own(self):
            self.phase1()
            for i in (2, 1, 3):
                for half in range(2):
                    go(lambda half=half, i=i: self.copy(2 + half, i, self.tile(half)))

        def forward(self):
            for k, i in enumerate((1, 3, 2)):
                for half in range(2):
                    self.one[half, i]().wait_recv()
                    back = {"dx": 4 - i} if half == 0 else {"dz": 4 - i}
                    for to in (2, 1, 3):
                        go(
                            lambda half=half, to=to, back=back, k=k: self.copy(
                                2 + half, to, self.tile(half, **back), 1 + k
                            )
                        )

        def done(self, halves=(0, 1), peers=(1, 3, 2)):
            for half in halves:
                for i in peers:
                    self.copy(2 + half, i, self.line(half)).wait_recv()

    def slice_of(d):
        return lax.rem(y + d, 4) * 2 + core

    def y_tiles(t):
        copies = {}
        for e in (2, 1, 3):
            rows = 128 if e == 2 else NEAR[t]
            if not rows:
                continue

            def make(e=e, rows=rows):
                piece = ybuf.at[t, row, z, x, pl.ds(0, rows)]
                return send(piece, piece, yt_ss.at[t, e - 1], yt_rs.at[t, e - 1], at(dy=e))

            copies[e] = go(make)
        return copies

    def y_line(t, back):
        for e in (1, 3):

            def make(e=e):
                piece = ybuf.at[t, row, :, lax.rem(x + 4 - back, 4), pl.ds(64, 64)]
                return send(piece, piece, yd_ss.at[t, e // 2, back], yd_rs.at[t, e // 2], at(dy=e))

            go(make)

    def y_line_wait(t, e):
        piece = ybuf.at[t, row, :, :, pl.ds(64, 64)]
        send(piece, piece, yd_ss.at[t, e // 2, 0], yd_rs.at[t, e // 2], at(dy=e)).wait_recv()

    def y_rest(t):
        copies = {}
        if NEAR[t] < 64:
            for e in (1, 3):

                def make(e=e):
                    piece = ybuf.at[t, row, :, :, pl.ds(NEAR[t], 64 - NEAR[t])]
                    return send(piece, piece, yr_ss.at[t, e // 2], yr_rs.at[t, e // 2], at(dy=e))

                copies[e] = go(make)
        return copies

    def across_copy(t, d, h):
        piece = ybuf.at[t, slice_of(d), :, :, pl.ds(64 * h, 64)]
        return send(piece, piece, cc_ss.at[t, d, h], cc_rs.at[t, d, h], at(other=True))

    def across(t, d, h):
        go(lambda: across_copy(t, d, h))

    def crossed(t, d, h):
        across_copy(t, d, h).wait_recv()

    def own_lines(t, gather, peers):
        for i in peers:
            gather.done((1,), (i,))
            y_line(t, i)

    own = [Gather(2 + t, ybuf.at[t, row], 0, 128) for t in range(2)]
    far = [
        {
            d: Gather(4 + 3 * t + d - 1, ybuf.at[t, slice_of(d)], 0, 128 if d == 2 else NEAR[t])
            for d in (2, 1, 3)
            if d == 2 or NEAR[t]
        }
        for t in range(2)
    ]
    g_b, g_f = Gather(0, b0, 0, 128), Gather(1, b1, 0, 128)

    def arrived(t, d, h):
        if d == 2:
            far[t][2].done((h,))
        elif h == 1:
            y_line_wait(t, 4 - d)
        else:
            if d in far[t]:
                far[t][d].done()
            if NEAR[t] < 64:
                rest[t][4 - d]().wait_recv()
        across(t, d, h)

    d_load.wait()
    b0_send(0).wait_recv()
    g_b.own()
    g_b.forward()

    @pl.when(row == 1)
    def _():
        for r, h in l10_parts[:2]:
            l10_send(r, h).wait_send()
        for r, h in l10_parts[2:]:
            l10_send(r, h).start()

    for a in range(5, 7):
        convert(a)
    d0 = split(dbuf[0])

    half = l10.at[core]
    l10_on = send(half, half, l_ss.at[1, 1], l_rs.at[core], (4 + core, col))
    l10_across = send(half, half, l_ss.at[1, 0], l_rs.at[core], at(other=True))
    first = jnp.logical_or(row == 2, row == 7)

    @pl.when(first)
    def _():
        l10_on.wait_recv()
        l10_on.start()
        l10_across.start()

    g_b.done()
    ybuf[0, row, z, x] = dot3(d0, split(b0[...].reshape(2048, 128)))
    own[0].own()
    tiles0 = y_tiles(0)

    own[0].forward()
    y_line(0, 0)

    own_lines(0, own[0], (1, 3))
    @pl.when(jnp.logical_and(y > 0, jnp.logical_not(first)))
    def _():
        l10_across.wait_recv()
        l10_across.start()

    @pl.when(y > 0)
    def _():
        send(half, l10.at[1 - core], l_ss.at[1, 0], l_rs.at[1 - core], at(other=True)).wait_recv()

    @pl.when(y == 0)
    def _():
        for h in range(2):
            send(l10.at[h], l10.at[h], l_ss.at[1, 0], l_rs.at[h], at(other=True)).wait_recv()

    send(b1_tile, b1_tile, s_ss.at[0], s_rs.at[1], (row, col)).wait_recv()
    lower = [split(l10[h]) for h in range(2)]
    own_lines(0, own[0], (2,))
    own[0].done((0,))

    mine = ybuf[0, row].reshape(2048, 128)
    b1[z, x] = b1_tile[...] - (dot3(lower[0], split(mine[:1024])) + dot3(lower[1], split(mine[1024:])))
    g_f.own()
    across(0, 0, 0)
    across(0, 0, 1)
    rest = [y_rest(0), {}]
    tiles0[2]().wait_recv()
    far[0][2].own()
    g_f.forward()
    far[0][2].forward()
    out_load.wait()

    def solve_second():
        arrived(0, 1, 1)
        arrived(0, 3, 1)
        d1 = split(dbuf[1])
        g_f.done()
        ybuf[1, row, z, x] = dot3(d1, split(b1[...].reshape(2048, 128)))
        second_tiles.update(y_tiles(1))
        own[1].own()
        crossed(0, 1, 1)

    second_tiles = {}

    def start_far():
        own[1].forward()
        y_line(1, 0)
        second_tiles[2]().wait_recv()
        far[1][2].own()
        for d in (1, 3):
            second_tiles[4 - d]().wait_recv()
            far[1][d].phase1()
        arrived(0, 2, 0)
        arrived(0, 2, 1)
        crossed(0, 2, 0)

    def forward_far():
        own_lines(1, own[1], (1, 3))
        far[1][2].forward()
        crossed(0, 2, 1)

    def second_gathered():
        own_lines(1, own[1], (2,))
        own[1].done((0,))
        across(1, 0, 0)
        across(1, 0, 1)
        far[1][1].phase2()
        far[1][3].phase2()
        arrived(0, 1, 0)
        arrived(0, 3, 0)
        crossed(0, 1, 0)

    def opposite():
        arrived(1, 2, 0)
        arrived(1, 2, 1)
        crossed(1, 0, 1)

    def near_high():
        arrived(1, 1, 1)
        arrived(1, 3, 1)
        crossed(1, 2, 1)

    def near_low():
        arrived(1, 1, 0)
        arrived(1, 3, 0)
        crossed(1, 1, 1)

    order = [(0, 0, 0), (0, 0, 1), (0, 1, 1), (0, 3, 1), (0, 2, 0), (0, 2, 1), (0, 1, 0), (0, 3, 0)]
    order += [(1, 0, 0), (1, 0, 1), (1, 2, 0), (1, 2, 1), (1, 1, 1), (1, 3, 1), (1, 1, 0), (1, 3, 0)]
    controls = {
        (0, 1, 1): solve_second,
        (0, 2, 0): start_far,
        (0, 2, 1): forward_far,
        (0, 1, 0): second_gathered,
        (1, 0, 1): opposite,
        (1, 2, 1): near_high,
        (1, 1, 1): near_low,
    }

    def job(k, carry):
        for i, unit in enumerate(order):
            pl.when(k == i)(controls.get(unit, lambda unit=unit: crossed(*unit)))

        def of(place):
            return sum((k == i).astype(jnp.int32) * unit[place] for i, unit in enumerate(order) if unit[place])

        t, d, h = of(0), of(1), of(2)
        q = lax.rem(y + d, 4)
        columns = pl.ds(pl.multiple_of(256 * q, 256), 256)
        for c in range(2):
            rows = ybuf[t, 2 * q + c, :, :, pl.ds(pl.multiple_of(64 * h, 64), 64), :]
            high, low = split(rows.reshape(1024, 128))
            yhi[:, 128 * c : 128 * c + 128] = high
            ylo[:, 128 * c : 128 * c + 128] = low
        out[:, columns] -= dot3((lhi[t, h], llo[t, h]), (yhi[...], ylo[...]))

        return carry

    lax.fori_loop(0, 16, job, 0)

    @pl.when(row < 2)
    def _():
        for r in range(8):
            out[0:128, 128 * r : 128 * r + 128] = ybuf[row, r, z, x]

    for make in sent:
        make().wait_send()

    @pl.when(row == 0)
    def _():
        for r in range(1, 8):
            b0_send(r).wait_send()

    @pl.when(row == 1)
    def _():
        for r in (0, 2, 3, 4, 5, 6, 7):
            b1_send(r).wait_send()
        for r, h in l10_parts[2:]:
            l10_send(r, h).wait_send()

    @pl.when(y > 0)
    def _():
        l10_across.wait_send()

    @pl.when(first)
    def _():
        l10_on.wait_send()


def on_device(lower_panel, test_cross, diag_inverse):
    V = pltpu.VMEM
    out = pl.pallas_call(
        kernel,
        out_shape=pltpu.VMEM((896, 1024), F32),
        in_specs=[pl.BlockSpec(memory_space=pl.ANY)] * 3,
        out_specs=pl.BlockSpec(memory_space=pltpu.VMEM),
        scratch_shapes=[
            V((2, 2, 896, 1024), BF16),
            V((2, 2, 896, 1024), BF16),
            V((2, 128, 4096), F32),
            V((2, 128, 2048), F32),
            V((2, 128, 1024), F32),
            V((4, 4, 128, 128), F32),
            V((4, 4, 128, 128), F32),
            V((128, 128), F32),
            V((2, 8, 4, 4, 128, 128), F32),
            V((1024, 256), BF16),
            V((1024, 256), BF16),
            DMA((2,)), DMA((2,)),
            DMA((8,)), DMA((2,)), DMA((8, 2)), DMA((2,)),
            DMA((10, 4, 3, 4)), DMA((10, 4, 3)),
            DMA((2, 3)), DMA((2, 3)), DMA((2, 2, 4)), DMA((2, 2)), DMA((2, 2)), DMA((2, 2)),
            DMA((2, 4, 2)), DMA((2, 4, 2)),
        ],
        compiler_params=pltpu.CompilerParams(
            collective_id=0, has_side_effects=True, vmem_limit_bytes=54 * 2**20
        ),
        cost_estimate=pl.CostEstimate(flops=22 * 10**9, bytes_accessed=24 * 10**6, transcendentals=0),
    )(lower_panel, test_cross.reshape(896, 1024), diag_inverse)
    return out.reshape(test_cross.shape)


def solution(mesh):
    placed = (P(None, "row", "col", None), P(None, "row", "col", None), P(None, "col", None))
    return jax.shard_map(
        on_device,
        mesh=mesh,
        in_specs=placed,
        out_specs=P(None, "row", "col", None),
        check_vma=False,
    )
```

```python
import jax
import jax.numpy as jnp
from jax import lax
from jax.experimental import pallas as pl
from jax.experimental.pallas import tpu as pltpu
from jax.sharding import PartitionSpec as P

MESH = pl.DeviceIdType.MESH
DMA = pltpu.SemaphoreType.DMA
F32 = jnp.float32
BF16 = jnp.bfloat16
NEAR = (0, 64)


def split(value):
    high = value.astype(BF16)
    return high, (value - high.astype(F32)).astype(BF16)


def dot3(a, b):
    def dot(u, v):
        return jnp.dot(u, v, preferred_element_type=F32)

    return dot(a[0], b[0]) + (dot(a[0], b[1]) + dot(a[1], b[0]))


def kernel(
    panel, cross, diag, out,
    lhi, llo, stage, dbuf, l10, b0, b1, b1_tile, ybuf, yhi, ylo,
    load_sem, stage_sem,
    s_ss, s_rs, l_ss, l_rs, pg_ss, pg_rs, yt_ss, yt_rs, yd_ss, yd_rs, yr_ss, yr_rs, cc_ss, cc_rs,
):
    row, col = lax.axis_index("row"), lax.axis_index("col")
    y, core = lax.div(row, 2), lax.rem(row, 2)
    z, x = lax.div(col, 4), lax.rem(col, 4)

    def at(dy=0, dz=0, dx=0, other=False):
        c = 1 - core if other else core
        return (lax.rem(y + dy, 4) * 2 + c, lax.rem(z + dz, 4) * 4 + lax.rem(x + dx, 4))

    def send(src, dst, ss, rs, device):
        return pltpu.make_async_remote_copy(
            src_ref=src, dst_ref=dst, send_sem=ss, recv_sem=rs, device_id=device, device_id_type=MESH
        )

    sent = []

    def go(make):
        make().start()
        sent.append(make)
        return make

    barrier = pltpu.get_barrier_semaphore()
    partners = [at(dx=i) for i in (1, 2, 3)] + [at(dz=i) for i in (1, 2, 3)]
    partners += [at(dy=i, other=o) for i in range(4) for o in (False, True) if i or o]
    for device in partners:
        pl.semaphore_signal(barrier, inc=1, device_id=device, device_id_type=MESH)

    d_load = pltpu.make_async_copy(diag, dbuf, load_sem.at[0])
    d_load.start()
    l_loads = [
        pltpu.make_async_copy(panel.at[a, 0], stage.at[a % 2], stage_sem.at[a % 2]) for a in range(7)
    ]
    l_loads[0].start()
    l_loads[1].start()
    out_load = pltpu.make_async_copy(cross, out, load_sem.at[1])
    out_load.start()

    def convert(a):
        l_loads[a].wait()

        def some_rows(g, carry):
            rows = pl.ds(pl.multiple_of(16 * g, 16), 16)
            to = pl.ds(pl.multiple_of(128 * a + 16 * g, 16), 16)
            left = lax.broadcasted_iota(jnp.int32, (16, 128), 1) < 64
            for t in range(2):
                for p in range(8):
                    one = stage[a % 2, rows, 2048 * t + 256 * p : 2048 * t + 256 * p + 128]
                    two = stage[a % 2, rows, 2048 * t + 256 * p + 128 : 2048 * t + 256 * p + 256]
                    parts = (
                        jnp.where(left, one, pltpu.roll(two, 64, 1)),
                        jnp.where(left, pltpu.roll(one, 64, 1), two),
                    )
                    for h in range(2):
                        high, low = split(parts[h])
                        lhi[t, h, to, 128 * p : 128 * p + 128] = high
                        llo[t, h, to, 128 * p : 128 * p + 128] = low
            return carry

        lax.fori_loop(0, 8, some_rows, 0)
        if a + 2 < 7:
            l_loads[a + 2].start()

    for a in range(2):
        convert(a)
    pl.semaphore_wait(barrier, len(partners))

    def tile_of(r):
        return cross.at[pl.ds(0, 128), pl.ds(128 * r, 128)]

    def b0_send(r):
        return send(tile_of(r), b0.at[z, x], s_ss.at[r], s_rs.at[0], (r, col))

    def b1_send(r):
        return send(tile_of(r), b1_tile, s_ss.at[r], s_rs.at[1], (r, col))

    def l10_half(h):
        return panel.at[0, 0, :, pl.ds(1024 * h, 1024)]

    def l10_send(r, h):
        return send(l10_half(h), l10.at[h], l_ss.at[r, h], l_rs.at[h], (r, col))

    l10_parts = [(2, 0), (7, 1), (3, 1), (6, 0), (0, 0), (0, 1)]

    @pl.when(row == 0)
    def _():
        for r in (4, 5, 2, 3, 6, 7, 1):
            b0_send(r).start()
        pltpu.make_async_copy(tile_of(0), b0.at[z, x], s_rs.at[0]).start()

    for a in range(2, 5):
        convert(a)

    @pl.when(row == 1)
    def _():
        for r, h in l10_parts[:2]:
            l10_send(r, h).start()
        for r in (4, 5, 2, 3, 6, 7, 0):
            b1_send(r).start()
        pltpu.make_async_copy(tile_of(1), b1_tile, s_rs.at[1]).start()
        for h in range(2):
            pltpu.make_async_copy(l10_half(h), l10.at[h], l_rs.at[h]).start()

    class Gather:
        def __init__(self, number, view, lo, hi):
            self.number, self.view = number, view
            mid = (lo + hi) // 2
            self.rows = (lo, mid - lo), (mid, hi - mid)

        def tile(self, half, dz=0, dx=0):
            return self.view.at[lax.rem(z + dz, 4), lax.rem(x + dx, 4), pl.ds(*self.rows[half])]

        def line(self, half):
            if half == 0:
                return self.view.at[z, :, pl.ds(*self.rows[half])]
            return self.view.at[:, x, pl.ds(*self.rows[half])]

        def copy(self, kind, i, piece, part=0):
            device = at(dx=i) if kind in (0, 3) else at(dz=i)
            ss, rs = pg_ss.at[self.number, kind, i - 1, part], pg_rs.at[self.number, kind, i - 1]
            return send(piece, piece, ss, rs, device)

        def phase1(self):
            self.one = {}
            for i in (2, 1, 3):
                for half in range(2):
                    self.one[half, i] = go(lambda half=half, i=i: self.copy(half, i, self.tile(half)))

        def phase2(self):
            for half, i in self.one:
                self.one[half, i]().wait_recv()
            for i in (2, 1, 3):
                for half in range(2):
                    go(lambda half=half, i=i: self.copy(2 + half, i, self.line(half)))

        def own(self):
            self.phase1()
            for i in (2, 1, 3):
                for half in range(2):
                    go(lambda half=half, i=i: self.copy(2 + half, i, self.tile(half)))

        def forward(self):
            for k, i in enumerate((1, 3, 2)):
                for half in range(2):
                    self.one[half, i]().wait_recv()
                    back = {"dx": 4 - i} if half == 0 else {"dz": 4 - i}
                    for to in (2, 1, 3):
                        go(
                            lambda half=half, to=to, back=back, k=k: self.copy(
                                2 + half, to, self.tile(half, **back), 1 + k
                            )
                        )

        def done(self, halves=(0, 1), peers=(1, 3, 2)):
            for half in halves:
                for i in peers:
                    self.copy(2 + half, i, self.line(half)).wait_recv()

    def slice_of(d):
        return lax.rem(y + d, 4) * 2 + core

    def y_tiles(t):
        copies = {}
        for e in (2, 1, 3):
            rows = 128 if e == 2 else NEAR[t]
            if not rows:
                continue

            def make(e=e, rows=rows):
                piece = ybuf.at[t, row, z, x, pl.ds(0, rows)]
                return send(piece, piece, yt_ss.at[t, e - 1], yt_rs.at[t, e - 1], at(dy=e))

            copies[e] = go(make)
        return copies

    def y_line(t, back):
        for e in (1, 3):

            def make(e=e):
                piece = ybuf.at[t, row, :, lax.rem(x + 4 - back, 4), pl.ds(64, 64)]
                return send(piece, piece, yd_ss.at[t, e // 2, back], yd_rs.at[t, e // 2], at(dy=e))

            go(make)

    def y_line_wait(t, e):
        piece = ybuf.at[t, row, :, :, pl.ds(64, 64)]
        send(piece, piece, yd_ss.at[t, e // 2, 0], yd_rs.at[t, e // 2], at(dy=e)).wait_recv()

    def y_rest(t):
        copies = {}
        if NEAR[t] < 64:
            for e in (1, 3):

                def make(e=e):
                    piece = ybuf.at[t, row, :, :, pl.ds(NEAR[t], 64 - NEAR[t])]
                    return send(piece, piece, yr_ss.at[t, e // 2], yr_rs.at[t, e // 2], at(dy=e))

                copies[e] = go(make)
        return copies

    def across_copy(t, d, h):
        piece = ybuf.at[t, slice_of(d), :, :, pl.ds(64 * h, 64)]
        return send(piece, piece, cc_ss.at[t, d, h], cc_rs.at[t, d, h], at(other=True))

    def across(t, d, h):
        go(lambda: across_copy(t, d, h))

    def crossed(t, d, h):
        across_copy(t, d, h).wait_recv()

    def own_lines(t, gather, peers):
        for i in peers:
            gather.done((1,), (i,))
            y_line(t, i)

    own = [Gather(2 + t, ybuf.at[t, row], 0, 128) for t in range(2)]
    far = [
        {
            d: Gather(4 + 3 * t + d - 1, ybuf.at[t, slice_of(d)], 0, 128 if d == 2 else NEAR[t])
            for d in (2, 1, 3)
            if d == 2 or NEAR[t]
        }
        for t in range(2)
    ]
    g_b, g_f = Gather(0, b0, 0, 128), Gather(1, b1, 0, 128)

    def arrived(t, d, h):
        if d == 2:
            far[t][2].done((h,))
        elif h == 1:
            y_line_wait(t, 4 - d)
        else:
            if d in far[t]:
                far[t][d].done()
            if NEAR[t] < 64:
                rest[t][4 - d]().wait_recv()
        across(t, d, h)

    d_load.wait()
    b0_send(0).wait_recv()
    g_b.own()
    g_b.forward()

    @pl.when(row == 1)
    def _():
        for r, h in l10_parts[:2]:
            l10_send(r, h).wait_send()
        for r, h in l10_parts[2:]:
            l10_send(r, h).start()

    for a in range(5, 7):
        convert(a)
    d0 = split(dbuf[0])

    half = l10.at[core]
    l10_on = send(half, half, l_ss.at[1, 1], l_rs.at[core], (4 + core, col))
    l10_across = send(half, half, l_ss.at[1, 0], l_rs.at[core], at(other=True))
    first = jnp.logical_or(row == 2, row == 7)

    @pl.when(first)
    def _():
        l10_on.wait_recv()
        l10_on.start()
        l10_across.start()

    g_b.done()
    ybuf[0, row, z, x] = dot3(d0, split(b0[...].reshape(2048, 128)))
    own[0].own()
    tiles0 = y_tiles(0)

    own[0].forward()
    y_line(0, 0)

    own_lines(0, own[0], (1, 3))
    @pl.when(jnp.logical_and(y > 0, jnp.logical_not(first)))
    def _():
        l10_across.wait_recv()
        l10_across.start()

    @pl.when(y > 0)
    def _():
        send(half, l10.at[1 - core], l_ss.at[1, 0], l_rs.at[1 - core], at(other=True)).wait_recv()

    @pl.when(y == 0)
    def _():
        for h in range(2):
            send(l10.at[h], l10.at[h], l_ss.at[1, 0], l_rs.at[h], at(other=True)).wait_recv()

    send(b1_tile, b1_tile, s_ss.at[0], s_rs.at[1], (row, col)).wait_recv()
    lower = [split(l10[h]) for h in range(2)]
    own_lines(0, own[0], (2,))
    own[0].done((0,))

    mine = ybuf[0, row].reshape(2048, 128)
    b1[z, x] = b1_tile[...] - (dot3(lower[0], split(mine[:1024])) + dot3(lower[1], split(mine[1024:])))
    g_f.own()
    across(0, 0, 0)
    across(0, 0, 1)
    rest = [y_rest(0), {}]
    tiles0[2]().wait_recv()
    far[0][2].own()
    g_f.forward()
    far[0][2].forward()
    out_load.wait()

    def solve_second():
        arrived(0, 1, 1)
        arrived(0, 3, 1)
        d1 = split(dbuf[1])
        g_f.done()
        ybuf[1, row, z, x] = dot3(d1, split(b1[...].reshape(2048, 128)))
        second_tiles.update(y_tiles(1))
        own[1].own()
        crossed(0, 1, 1)

    second_tiles = {}

    gone = []

    def start_far():
        gone.extend(sent)
        sent.clear()
        own[1].forward()
        y_line(1, 0)
        second_tiles[2]().wait_recv()
        far[1][2].own()
        for d in (1, 3):
            second_tiles[4 - d]().wait_recv()
            far[1][d].phase1()
        arrived(0, 2, 0)
        arrived(0, 2, 1)
        crossed(0, 2, 0)

    def forward_far():
        own_lines(1, own[1], (1, 3))
        far[1][2].forward()
        crossed(0, 2, 1)

    def second_gathered():
        own_lines(1, own[1], (2,))
        own[1].done((0,))
        across(1, 0, 0)
        across(1, 0, 1)
        far[1][1].phase2()
        far[1][3].phase2()
        arrived(0, 1, 0)
        arrived(0, 3, 0)
        crossed(0, 1, 0)

    def opposite():
        for make in gone:
            make().wait_send()
        arrived(1, 2, 0)
        arrived(1, 2, 1)
        crossed(1, 0, 1)

    def near_high():
        arrived(1, 1, 1)
        arrived(1, 3, 1)
        crossed(1, 2, 1)

    def near_low():
        arrived(1, 1, 0)
        arrived(1, 3, 0)
        crossed(1, 1, 1)

    order = [(0, 0, 0), (0, 0, 1), (0, 1, 1), (0, 3, 1), (0, 2, 0), (0, 2, 1), (0, 1, 0), (0, 3, 0)]
    order += [(1, 0, 0), (1, 0, 1), (1, 2, 0), (1, 2, 1), (1, 1, 1), (1, 3, 1), (1, 1, 0), (1, 3, 0)]
    controls = {
        (0, 1, 1): solve_second,
        (0, 2, 0): start_far,
        (0, 2, 1): forward_far,
        (0, 1, 0): second_gathered,
        (1, 0, 1): opposite,
        (1, 2, 1): near_high,
        (1, 1, 1): near_low,
    }

    def job(k, carry):
        for i, unit in enumerate(order):
            pl.when(k == i)(controls.get(unit, lambda unit=unit: crossed(*unit)))

        def of(place):
            return sum((k == i).astype(jnp.int32) * unit[place] for i, unit in enumerate(order) if unit[place])

        t, d, h = of(0), of(1), of(2)
        q = lax.rem(y + d, 4)
        columns = pl.ds(pl.multiple_of(256 * q, 256), 256)
        for c in range(2):
            rows = ybuf[t, 2 * q + c, :, :, pl.ds(pl.multiple_of(64 * h, 64), 64), :]
            high, low = split(rows.reshape(1024, 128))
            yhi[:, 128 * c : 128 * c + 128] = high
            ylo[:, 128 * c : 128 * c + 128] = low
        out[:, columns] -= dot3((lhi[t, h], llo[t, h]), (yhi[...], ylo[...]))

        return carry

    lax.fori_loop(0, 16, job, 0)

    @pl.when(row < 2)
    def _():
        for r in range(8):
            out[0:128, 128 * r : 128 * r + 128] = ybuf[row, r, z, x]

    for make in sent:
        make().wait_send()

    @pl.when(row == 0)
    def _():
        for r in range(1, 8):
            b0_send(r).wait_send()

    @pl.when(row == 1)
    def _():
        for r in (0, 2, 3, 4, 5, 6, 7):
            b1_send(r).wait_send()
        for r, h in l10_parts[2:]:
            l10_send(r, h).wait_send()

    @pl.when(y > 0)
    def _():
        l10_across.wait_send()

    @pl.when(first)
    def _():
        l10_on.wait_send()


def on_device(lower_panel, test_cross, diag_inverse):
    V = pltpu.VMEM
    out = pl.pallas_call(
        kernel,
        out_shape=pltpu.VMEM((896, 1024), F32),
        in_specs=[pl.BlockSpec(memory_space=pl.ANY)] * 3,
        out_specs=pl.BlockSpec(memory_space=pltpu.VMEM),
        scratch_shapes=[
            V((2, 2, 896, 1024), BF16),
            V((2, 2, 896, 1024), BF16),
            V((2, 128, 4096), F32),
            V((2, 128, 2048), F32),
            V((2, 128, 1024), F32),
            V((4, 4, 128, 128), F32),
            V((4, 4, 128, 128), F32),
            V((128, 128), F32),
            V((2, 8, 4, 4, 128, 128), F32),
            V((1024, 256), BF16),
            V((1024, 256), BF16),
            DMA((2,)), DMA((2,)),
            DMA((8,)), DMA((2,)), DMA((8, 2)), DMA((2,)),
            DMA((10, 4, 3, 4)), DMA((10, 4, 3)),
            DMA((2, 3)), DMA((2, 3)), DMA((2, 2, 4)), DMA((2, 2)), DMA((2, 2)), DMA((2, 2)),
            DMA((2, 4, 2)), DMA((2, 4, 2)),
        ],
        compiler_params=pltpu.CompilerParams(
            collective_id=0, has_side_effects=True, vmem_limit_bytes=54 * 2**20
        ),
        cost_estimate=pl.CostEstimate(flops=22 * 10**9, bytes_accessed=24 * 10**6, transcendentals=0),
    )(lower_panel, test_cross.reshape(896, 1024), diag_inverse)
    return out.reshape(test_cross.shape)


def solution(mesh):
    placed = (P(None, "row", "col", None), P(None, "row", "col", None), P(None, "col", None))
    return jax.shard_map(
        on_device,
        mesh=mesh,
        in_specs=placed,
        out_specs=P(None, "row", "col", None),
        check_vma=False,
    )
```
